128 devices in a mesh: row: 8 (over y, x_hi), col: 16 (over x_lo, z, core).
Axes of the slice: x: 4 (x_hi: 2, x_lo: 2; x = x_hi * 2 + x_lo), y: 4, z: 4, core: 2. Of those that a mesh axis runs over, the one named last changes fastest.
Arguments:
- weight: bfloat16 [4096, 8192], P('row', 'col'), may hold values from -0.4375 to 0.4375
- anchor: bfloat16 [4096, 8192], P('row', 'col'), may hold values from -0.4375 to 0.4375
- input_factor: bfloat16 [8192, 8192], P('row', 'col'), may hold values from -2 to 50
- output_factor: bfloat16 [4096, 4096], P('row', 'col'), may hold values from -8 to 200
- task_grad: bfloat16 [4096, 8192], P(('row', 'col')), may hold values from -6 to 6
Outputs:
- updated_grad: bfloat16 [4096, 8192], P(('row', 'col'))
The draws below stay inside these ranges and needn't reach their ends.
All inputs are finite; a program needn't handle non-finite values.
Results may differ from the reference program's by a relative error of at most 0.0059.
Values may be sent and summed in bfloat16 or wider, within the bound.
No kernel may reach another device: no remote copies, remote signals or barrier semaphores. Data moves between devices by JAX's collectives and lax.ppermute only.
A program may use at most 64 MiB of HBM per device.

```python
import math
import jax
import jax.numpy as jnp

D_IN = 8192
D_OUT = 4096


def build_factor(diag_vals, noise, spread):
    size = diag_vals.shape[0]
    symmetric = (noise + noise.T) * (0.7071068 * spread / math.sqrt(size))
    matrix = symmetric + jnp.diag(diag_vals)
    return matrix


def draw_input_factor(key, part):
    key = jax.random.fold_in(key, 11)
    diag_key, noise_key = jax.random.split(key, 2)
    diag_vals = jax.random.uniform(diag_key, (D_IN,), jnp.float32, 1.0, 3.0)
    noise = jnp.clip(jax.random.normal(noise_key, (D_IN, D_IN), jnp.float32), -6.0, 6.0)
    return build_factor(diag_vals, noise, 0.45).astype(jnp.bfloat16)


def draw_output_factor(key, part):
    key = jax.random.fold_in(key, 23)
    diag_key, noise_key = jax.random.split(key, 2)
    diag_vals = jax.random.uniform(diag_key, (D_OUT,), jnp.float32, 4.0, 12.0)
    noise = jnp.clip(jax.random.normal(noise_key, (D_OUT, D_OUT), jnp.float32), -6.0, 6.0)
    return build_factor(diag_vals, noise, 1.8).astype(jnp.bfloat16)


def level_of(stream_key, extent, cuts, smallest, largest):
    gain, own = 1.0, jax.random.fold_in(stream_key, 6)
    for position, shards_of in cuts:
        steps = jnp.exp(jax.random.uniform(jax.random.fold_in(own, position), (shards_of,), jnp.float32, smallest / len(cuts), largest / len(cuts)))
        gain = gain * jnp.repeat(steps, extent[position] // shards_of).reshape([-1 if axis == position else 1 for axis in range(len(extent))])
    return gain


def centred(own_key, extent, width, limit, pieces=(), kind=jnp.bfloat16):
    result = jax.random.normal(own_key, extent, jnp.float32) * width
    if len(pieces) > 0:
        result = level_of(own_key, extent, pieces, -0.22, 0.18) * result
    return jnp.clip(result, min=-limit, max=limit).astype(kind)


def setup_inputs(seed: int = 0) -> dict:
    seeds = jax.random.split(jax.random.key(seed), 6)
    weight = centred(seeds[0], (D_OUT, D_IN), 0.03, 0.4375, ((0, 8), (1, 16)))
    anchor = centred(seeds[1], (D_OUT, D_IN), 0.03, 0.4375, ((0, 8), (1, 16)))
    input_factor = draw_input_factor(jax.random.fold_in(seeds[5], 71), 0)
    output_factor = draw_output_factor(jax.random.fold_in(seeds[5], 71), 0)
    task_grad = centred(seeds[4], (D_OUT, D_IN), 0.5, 6.0, ((0, 128),))
    return {"weight": weight, "anchor": anchor, "input_factor": input_factor, "output_factor": output_factor, "task_grad": task_grad}


def reference(weight, anchor, input_factor, output_factor, task_grad):
    change = (weight.astype(jnp.float32) - anchor.astype(jnp.float32)).astype(jnp.bfloat16)
    projected = jnp.dot(change, input_factor, preferred_element_type=jnp.float32).astype(jnp.bfloat16)
    penalty = jnp.dot(output_factor, projected, preferred_element_type=jnp.float32)
    return (task_grad.astype(jnp.float32) + penalty).astype(jnp.bfloat16)
```

```python
import jax
import jax.numpy as jnp
from jax import lax
from jax.sharding import Mesh, PartitionSpec as P

ROW = ("y", "xh")
COL = ("xl", "z", "core")
F32, BF16 = jnp.float32, jnp.bfloat16


def shift(v, axis, by):
    n = lax.axis_size(axis)
    return lax.ppermute(v, axis, [(i, (i + by) % n) for i in range(n)])


def turn(v):
    pairs = [(xh * 4 + z, (z & 1) * 4 + (z & ~1) + xh) for xh in range(2) for z in range(4)]
    return lax.ppermute(v, ("xh", "z"), pairs)


def ring(v, axis):
    half = v.shape[0] // 2
    below, above = shift(v, axis, 1), shift(v, axis, -1)
    far = [shift(below[:half], axis, 1), shift(above[half:], axis, -1)]
    return below, above, jnp.concatenate(far, axis=0)


def across(v):
    half = v.shape[0] // 2
    up, down = v[:half], v[half:]
    for _ in range(2):
        up, down = shift(up, ("xh", "xl"), 1), shift(down, ("xh", "xl"), -1)
    return jnp.concatenate([up, down], axis=0)


def dot(a, b):
    return jnp.dot(a, b, preferred_element_type=F32)


def body(weight, anchor, input_factor, output_factor, task_grad):
    y, xh, xl, z, core = (lax.axis_index(a) for a in ROW + COL)
    change = (weight.astype(F32) - anchor.astype(F32)).astype(BF16)

    depth = input_factor.shape[0] // 2
    mine = lax.dynamic_slice_in_dim(input_factor, core * depth, depth, 0)
    other = lax.dynamic_slice_in_dim(input_factor, (1 - core) * depth, depth, 0)
    pair = jnp.concatenate([mine, shift(other, "core", 1)], axis=1)
    factor = lax.all_gather(pair, "y", axis=0, tiled=True)

    a = turn(change)
    am, ap, a2 = ring(a, "z")
    b = shift(a, "xl", 1)
    bm, bp = shift(b, "z", 1), shift(b, "z", -1)
    b2 = shift(a2, "xl", 1)

    out_turned = turn(output_factor)
    out_cols = lax.all_gather(out_turned, COL, axis=0)

    def term(block, dxl, dz):
        at = ((xl + dxl) % 2) * 2 + ((z + dz) % 4) // 2
        return dot(block, lax.dynamic_slice_in_dim(factor, at * depth, depth, 0))

    even = term(a, 0, 0) + term(a2, 0, 2) + term(b, 1, 0) + term(b2, 1, 2)
    odd = term(am, 0, -1) + term(ap, 0, 1) + term(bm, 1, -1) + term(bp, 1, 1)
    same = (z % 2) == xh
    keep = jnp.where(same, even, odd)
    send = jnp.where(same, odd, even)
    cols = weight.shape[1]
    theirs = jnp.concatenate([send[:, cols:], keep[:, cols:]], axis=0).astype(BF16)
    got = shift(theirs, "core", 1).astype(F32)
    rows = weight.shape[0]
    send = (send[:, :cols] + got[:rows]).astype(BF16)
    keep = keep[:, :cols] + got[rows:]
    projected = (keep + across(send).astype(F32)).astype(BF16)

    pm, pp, p2 = ring(projected, "y")
    n = output_factor.shape[1]
    left = out_cols.reshape(4, 2, 2, rows, n).transpose(0, 1, 3, 2, 4).reshape(4, 2 * rows, 2 * n)

    def share(block, dy):
        return dot(lax.dynamic_index_in_dim(left, (y + dy) % 4, 0, keepdims=False), block)

    penalty = share(projected, 0) + share(pm, -1) + share(pp, 1) + share(p2, 2)
    owned = lax.all_to_all(penalty.astype(BF16), ("xh",) + COL, split_axis=0, concat_axis=0, tiled=True)
    owned = owned.reshape(2, 16, task_grad.shape[0], cols).astype(F32).sum(axis=0)
    owned = owned.transpose(1, 0, 2).reshape(task_grad.shape)
    return (task_grad.astype(F32) + owned).astype(BF16)


def solution(mesh):
    fine = Mesh(mesh.devices.reshape(4, 2, 2, 4, 2), ROW + COL)
    block = P(ROW, COL)
    placed = (block, block, block, block, P(ROW + COL, None))
    return jax.shard_map(
        body, mesh=fine, in_specs=placed, out_specs=P(ROW + COL, None), check_vma=False
    )
```

```python
import jax
import jax.numpy as jnp
from jax import lax
from jax.sharding import Mesh, PartitionSpec as P

ROW = ("y", "xh")
COL = ("xl", "z", "core")
F32, BF16 = jnp.float32, jnp.bfloat16


def shift(v, axis, by):
    n = lax.axis_size(axis)
    return lax.ppermute(v, axis, [(i, (i + by) % n) for i in range(n)])


def turn(v, flip):
    pairs = []
    for xh in range(2):
        for xl in range(2):
            for z in range(4):
                to = ((z & 1) * 2 + (xl ^ flip)) * 4 + (z & ~1) + xh
                pairs.append(((xh * 2 + xl) * 4 + z, to))
    return lax.ppermute(v, ("xh", "xl", "z"), pairs)


def after(v, *done):
    return lax.optimization_barrier((v, *done))[0]


def dot(a, b):
    return jnp.dot(a, b, preferred_element_type=F32)


def body(weight, anchor, input_factor, output_factor, task_grad):
    y, xh, xl, z, core = (lax.axis_index(a) for a in ROW + COL)
    change = (weight.astype(F32) - anchor.astype(F32)).astype(BF16)
    rows, cols = weight.shape

    a, b = turn(change, 0), turn(change, 1)

    depth = input_factor.shape[0] // 2
    mine = lax.dynamic_slice_in_dim(input_factor, core * depth, depth, 0)
    other = lax.dynamic_slice_in_dim(input_factor, (1 - core) * depth, depth, 0)
    pair = jnp.concatenate([mine, shift(other, "core", 1)], axis=1)
    below, above = shift(pair, "y", 1), shift(pair, "y", -1)
    far = [shift(below[: depth // 2], "y", 1), shift(above[depth // 2 :], "y", -1)]
    factor = jnp.concatenate([pair, above, *far, below], axis=0)

    am, bp = shift(a, "z", 1), shift(b, "z", -1)
    bm, ap = shift(b, "z", 1), shift(a, "z", -1)
    a2, b2 = shift(am, "z", 1), shift(bp, "z", -1)

    part = after(output_factor, am, bp)
    part = jnp.concatenate([turn(part, 0), turn(part, 1)], axis=0)
    left = lax.all_gather(part, ("z", "core"), axis=1, tiled=True)

    def term(block, dxl, dz):
        at = (xl ^ dxl) * 2 + (((z + dz) & 3) >> 1)
        return dot(block, lax.dynamic_slice_in_dim(factor, ((at - y) & 3) * depth, depth, 0))

    odd = term(am, 0, -1) + term(ap, 0, 1) + term(bm, 1, -1) + term(bp, 1, 1)
    even = term(a, 0, 0) + term(b, 1, 0) + term(a2, 0, 2) + term(b2, 1, 2)
    same = (z & 1) == xh
    keep = jnp.where(same, even, odd)
    send = jnp.where(same, odd, even)
    theirs = jnp.concatenate([send[:, cols:], keep[:, cols:]], axis=0).astype(BF16)
    got = shift(theirs, "core", 1).astype(F32)
    send = (send[:, :cols] + got[:rows]).astype(BF16)
    keep = keep[:, :cols] + got[rows:]
    projected = (keep + shift(send, "xh", 1).astype(F32)).astype(BF16)

    half = rows // 2
    pm, pp = shift(projected, "y", 1), shift(projected, "y", -1)
    p2 = jnp.concatenate([shift(pm[:half], "y", 1), shift(pp[half:], "y", -1)], axis=0)

    def share(block, dy, to):
        at = (y + dy) & 3
        corner = (((at >> 1) ^ xl) * rows, ((at & 1) * 2 + to) * rows)
        return dot(lax.dynamic_slice(left, corner, (rows, rows)), block)

    penalty = [
        share(projected, 0, to) + share(pm, -1, to) + share(pp, 1, to) + share(p2, 2, to)
        for to in range(2)
    ]
    penalty = jnp.concatenate(penalty, axis=0).astype(BF16)
    owned = lax.all_to_all(penalty, ("xh",) + COL, split_axis=0, concat_axis=0, tiled=True)
    owned = owned.reshape(2, 16, task_grad.shape[0], cols).astype(F32).sum(axis=0)
    owned = owned.transpose(1, 0, 2).reshape(task_grad.shape)
    return (task_grad.astype(F32) + owned).astype(BF16)


def solution(mesh):
    fine = Mesh(mesh.devices.reshape(4, 2, 2, 4, 2), ROW + COL)
    block = P(ROW, COL)
    placed = (block, block, block, block, P(ROW + COL, None))
    return jax.shard_map(
        body, mesh=fine, in_specs=placed, out_specs=P(ROW + COL, None), check_vma=False
    )
```

```python
import jax
import jax.numpy as jnp
from jax import lax
from jax.sharding import Mesh, PartitionSpec as P

ROW = ("y", "xh")
COL = ("xl", "z", "core")
F32, BF16 = jnp.float32, jnp.bfloat16


def shift(v, axis, by):
    n = lax.axis_size(axis)
    return lax.ppermute(v, axis, [(i, (i + by) % n) for i in range(n)])


def turn(v, flip):
    pairs = []
    for xh in range(2):
        for xl in range(2):
            for z in range(4):
                to = ((z & 1) * 2 + (xl ^ flip)) * 4 + (z & ~1) + xh
                pairs.append(((xh * 2 + xl) * 4 + z, to))
    return lax.ppermute(v, ("xh", "xl", "z"), pairs)


def after(v, *done):
    return lax.optimization_barrier((v, *done))[0]


def dot(a, b):
    return jnp.dot(a, b, preferred_element_type=F32)


def body(weight, anchor, input_factor, output_factor, task_grad):
    y, xh, xl, z, core = (lax.axis_index(a) for a in ROW + COL)
    change = (weight.astype(F32) - anchor.astype(F32)).astype(BF16)
    rows, cols = weight.shape

    a, b = turn(change, 0), turn(change, 1)

    depth = input_factor.shape[0] // 2
    mine = lax.dynamic_slice_in_dim(input_factor, core * depth, depth, 0)
    other = lax.dynamic_slice_in_dim(input_factor, (1 - core) * depth, depth, 0)
    pair = jnp.concatenate([mine, shift(other, "core", 1)], axis=1)
    factor = lax.all_gather(pair, "y", axis=0, tiled=True)

    am, bp = shift(a, "z", 1), shift(b, "z", -1)
    bm, ap = shift(b, "z", 1), shift(a, "z", -1)
    a2, b2 = shift(am, "z", 1), shift(bp, "z", -1)

    part = after(output_factor, am, ap, bm, bp)
    part = jnp.concatenate([turn(part, 0), turn(part, 1)], axis=0)
    left = lax.all_gather(part, ("z", "core"), axis=1, tiled=True)

    def term(block, dxl, dz):
        at = (xl ^ dxl) * 2 + (((z + dz) & 3) >> 1)
        return dot(block, lax.dynamic_slice_in_dim(factor, at * depth, depth, 0))

    odd = term(am, 0, -1) + term(ap, 0, 1) + term(bm, 1, -1) + term(bp, 1, 1)
    even = term(a, 0, 0) + term(b, 1, 0) + term(a2, 0, 2) + term(b2, 1, 2)
    same = (z & 1) == xh
    keep = jnp.where(same, even, odd)
    send = jnp.where(same, odd, even)
    theirs = jnp.concatenate([send[:, cols:], keep[:, cols:]], axis=0).astype(BF16)
    got = shift(theirs, "core", 1).astype(F32)
    send = (send[:, :cols] + got[:rows]).astype(BF16)
    keep = keep[:, :cols] + got[rows:]
    projected = (keep + shift(send, "xh", 1).astype(F32)).astype(BF16)

    half = rows // 2
    pm, pp = shift(projected, "y", 1), shift(projected, "y", -1)
    p2 = jnp.concatenate([shift(pm[:half], "y", 1), shift(pp[half:], "y", -1)], axis=0)

    def share(block, dy, to):
        at = (y + dy) & 3
        corner = (((at >> 1) ^ xl) * rows, ((at & 1) * 2 + to) * rows)
        return dot(lax.dynamic_slice(left, corner, (rows, rows)), block)

    penalty = [
        share(projected, 0, to) + share(pm, -1, to) + share(pp, 1, to) + share(p2, 2, to)
        for to in range(2)
    ]
    penalty = jnp.concatenate(penalty, axis=0).astype(BF16)
    owned = lax.all_to_all(penalty, ("xh",) + COL, split_axis=0, concat_axis=0, tiled=True)
    owned = owned.reshape(2, 16, task_grad.shape[0], cols).astype(F32).sum(axis=0)
    owned = owned.transpose(1, 0, 2).reshape(task_grad.shape)
    return (task_grad.astype(F32) + owned).astype(BF16)


def solution(mesh):
    fine = Mesh(mesh.devices.reshape(4, 2, 2, 4, 2), ROW + COL)
    block = P(ROW, COL)
    placed = (block, block, block, block, P(ROW + COL, None))
    return jax.shard_map(
        body, mesh=fine, in_specs=placed, out_specs=P(ROW + COL, None), check_vma=False
    )
```

```python
import jax
import jax.numpy as jnp
from jax import lax
from jax.experimental import pallas as pl
from jax.experimental.pallas import tpu as pltpu
from jax.sharding import Mesh, PartitionSpec as P

ROW = ("y", "xh")
COL = ("xl", "z", "core")
F32, BF16 = jnp.float32, jnp.bfloat16


def shift(v, axis, by):
    n = lax.axis_size(axis)
    return lax.ppermute(v, axis, [(i, (i + by) % n) for i in range(n)])


def turn(v):
    pairs = []
    for xh in range(2):
        for xl in range(2):
            for z in range(4):
                to = ((z & 1) * 2 + 1 - xl) * 4 + (z & ~1) + xh
                pairs.append(((xh * 2 + xl) * 4 + z, to))
    return lax.ppermute(v, ("xh", "xl", "z"), pairs)


def after(v, *done):
    return lax.optimization_barrier((v, *done))[0]


def together(*arrays):
    return lax.optimization_barrier(arrays)


def dot(a, b):
    return lax.dot_general(a, b, (((a.ndim - 1,), (0,)), ((), ())), preferred_element_type=F32)


def early_kernel(n, m, at, *refs):
    blocks, factor = refs[: n + m], refs[n + m]
    theirs, own, part, held, right, total, came = refs[n + m + 1 :]
    size, depth = blocks[0].shape
    cols = own.shape[1]
    rows = [pl.ds(pl.multiple_of(at[i] * depth, depth), depth) for i in range(n + m)]
    copies = []
    for i in range(n + m):
        copies.append([pltpu.make_async_copy(blocks[i], held.at[i], came.at[2 * i])])
        if i < n:
            copies[i].append(pltpu.make_async_copy(factor.at[rows[i]], right.at[rows[i]], came.at[2 * i + 1]))
    for copy in sum(copies, []):
        copy.start()
    step = min(256, cols)
    for lo, hi in ((0, n // 2), (n // 2, n), (n, n + m)):
        for copy in sum(copies[lo:hi], []):
            copy.wait()
        for c in range(0, 2 * cols, step):
            here = slice(c, c + step)
            value = None
            for i in range(lo, hi):
                more = dot(held[i], right[rows[i], here])
                value = more if value is None else value + more
            if lo == 0:
                total[:, here] = value
            elif hi > n:
                part[:, here] = value
            elif c < cols:
                own[:, here] = total[:, here] + value
            else:
                theirs[:, c - cols : c - cols + step] = (total[:, here] + value).astype(BF16)


def early(odd, even, factor, at):
    n, m = len(odd), len(even)
    size, depth = odd[0].shape
    wide = factor.shape[1]
    return pl.pallas_call(
        lambda *refs: early_kernel(n, m, *refs),
        out_shape=(
            jax.ShapeDtypeStruct((size, wide // 2), BF16),
            jax.ShapeDtypeStruct((size, wide // 2), F32),
            jax.ShapeDtypeStruct((size, wide), F32),
        ),
        in_specs=[pl.BlockSpec(memory_space=pltpu.SMEM)] + [pl.BlockSpec(memory_space=pl.ANY)] * (n + m + 1),
        out_specs=(pl.BlockSpec(memory_space=pltpu.VMEM),) * 3,
        scratch_shapes=[
            pltpu.VMEM((n + m, size, depth), BF16),
            pltpu.VMEM(factor.shape, BF16),
            pltpu.VMEM((size, wide), F32),
            pltpu.SemaphoreType.DMA((2 * (n + m),)),
        ],
        compiler_params=pltpu.CompilerParams(vmem_limit_bytes=56 * 2**20),
        cost_estimate=pl.CostEstimate(
            flops=2 * (n + m) * size * depth * wide, bytes_accessed=12 * 2**20, transcendentals=0
        ),
    )(jnp.stack(at).astype(jnp.int32), *odd, *even, factor)


def body(weight, anchor, input_factor, output_factor, task_grad):
    y, xh, xl, z, core = (lax.axis_index(a) for a in ROW + COL)
    change = (weight.astype(F32) - anchor.astype(F32)).astype(BF16)
    rows, cols = weight.shape
    half = rows // 2

    depth = input_factor.shape[0] // 2
    mine = lax.dynamic_slice_in_dim(input_factor, core * depth, depth, 0)
    other = lax.dynamic_slice_in_dim(input_factor, (1 - core) * depth, depth, 0)
    pair = jnp.concatenate([mine, shift(other, "core", 1)], axis=1)
    factor = lax.all_gather(pair, "y", axis=0, tiled=True)

    b = turn(change)
    bm, bp, a = together(shift(b, "z", 1), shift(b, "z", -1), shift(b, "xl", 1))
    am, ap, b2 = together(shift(bm, "xl", 1), shift(a, "z", -1), shift(bm, "z", 1))
    far = [shift(am[:half], "z", 1), shift(ap[half:], "z", -1)]
    *far, part = together(*far, turn(after(output_factor, am, ap, b2, factor)))

    def place(dxl, dz):
        return (xl ^ dxl) * 2 + (((z + dz) & 3) >> 1)

    at = [place(0, -1), place(0, 1), place(1, -1), place(1, 1), place(0, 0), place(1, 0), place(1, 2)]
    theirs, own, even = early([am, ap, bm, bp], [a, b, b2], factor, at)
    far_off = shift(after(part, own), "xl", 1)
    odd = own + shift(theirs, "core", 1).astype(F32)

    def more(side):
        right = lax.dynamic_slice(factor, (place(0, 2) * depth, side * cols), (depth, cols))
        last = jnp.concatenate([dot(v, right) for v in far], axis=0)
        return even[:, side * cols : (side + 1) * cols] + last

    theirs, own = more(1).astype(BF16), more(0)
    got = shift(theirs, "core", 1)
    part = jnp.concatenate([after(far_off, got), part], axis=0)
    part = lax.all_gather(part, "z", axis=0)
    even = got.astype(F32) + own
    same = (z & 1) == xh
    send = shift(jnp.where(same, odd, even).astype(BF16), "xh", 1)
    keep = jnp.where(same, even, odd)

    p = [(keep[r] + send[r].astype(F32)).astype(BF16) for r in (slice(half), slice(half, rows))]
    below = [shift(p[0], "y", 1), shift(p[1], "y", 1)]
    above = [shift(p[0], "y", -1), shift(p[1], "y", -1)]
    beyond = [shift(below[0], "y", 1), shift(above[1], "y", -1)]
    swapped = shift(after(part, *below, *above), "core", 1)
    first = core == 0
    left = [jnp.where(first, part, swapped), jnp.where(first, swapped, part)]

    def share(blocks, dy):
        at = (y + dy) & 3
        corner, size = ((at & 1) * 2, ((at >> 1) ^ xl) * rows, 0), (2, rows, half)
        terms = [dot(lax.dynamic_slice(v, corner, size), w) for v, w in zip(left, blocks)]
        return terms[0] + terms[1]

    penalty = ((share(p, 0) + share(below, -1)) + share(above, 1)) + share(beyond, 2)
    penalty = penalty.astype(BF16).reshape(2 * rows, cols)
    owned = lax.all_to_all(penalty, ("xh",) + COL, split_axis=0, concat_axis=0, tiled=True)
    owned = owned.reshape(2, 16, task_grad.shape[0], cols).astype(F32).sum(axis=0)
    owned = owned.transpose(1, 0, 2).reshape(task_grad.shape)
    return (task_grad.astype(F32) + owned).astype(BF16)


def solution(mesh):
    fine = Mesh(mesh.devices.reshape(4, 2, 2, 4, 2), ROW + COL)
    cut = P(ROW, COL)
    placed = (cut, cut, cut, cut, P(ROW + COL, None))
    return jax.shard_map(
        body, mesh=fine, in_specs=placed, out_specs=P(ROW + COL, None), check_vma=False
    )
```

```python
import jax
import jax.numpy as jnp
from jax import lax
from jax.experimental import pallas as pl
from jax.experimental.pallas import tpu as pltpu
from jax.sharding import Mesh, PartitionSpec as P

ROW = ("y", "xh")
COL = ("xl", "z", "core")
F32, BF16 = jnp.float32, jnp.bfloat16


def shift(v, axis, by):
    n = lax.axis_size(axis)
    return lax.ppermute(v, axis, [(i, (i + by) % n) for i in range(n)])


def turn(v):
    pairs = []
    for xh in range(2):
        for xl in range(2):
            for z in range(4):
                to = ((z & 1) * 2 + 1 - xl) * 4 + (z & ~1) + xh
                pairs.append(((xh * 2 + xl) * 4 + z, to))
    return lax.ppermute(v, ("xh", "xl", "z"), pairs)


def after(v, *done):
    return lax.optimization_barrier((v, *done))[0]


def together(*arrays):
    return lax.optimization_barrier(arrays)


def dot(a, b):
    return lax.dot_general(a, b, (((a.ndim - 1,), (0,)), ((), ())), preferred_element_type=F32)


def early_kernel(n, m, at, *refs):
    blocks, factor = refs[: n + m], refs[n + m]
    theirs, own, part, held, right, total, came = refs[n + m + 1 :]
    size, depth = blocks[0].shape
    cols = own.shape[1]
    rows = [pl.ds(pl.multiple_of(at[i] * depth, depth), depth) for i in range(n + m)]
    copies = []
    for i in range(n + m):
        copies.append([pltpu.make_async_copy(blocks[i], held.at[i], came.at[2 * i])])
        if i < n:
            copies[i].append(pltpu.make_async_copy(factor.at[rows[i]], right.at[rows[i]], came.at[2 * i + 1]))
    for copy in sum(copies, []):
        copy.start()
    step = min(256, cols)
    for lo, hi in ((0, n // 2), (n // 2, n), (n, n + m)):
        for copy in sum(copies[lo:hi], []):
            copy.wait()
        for c in range(0, 2 * cols, step):
            here = slice(c, c + step)
            value = None
            for i in range(lo, hi):
                more = dot(held[i], right[rows[i], here])
                value = more if value is None else value + more
            if lo == 0:
                total[:, here] = value
            elif hi > n:
                part[:, here] = value
            elif c < cols:
                own[:, here] = total[:, here] + value
            else:
                theirs[:, c - cols : c - cols + step] = (total[:, here] + value).astype(BF16)


def early(odd, even, factor, at):
    n, m = len(odd), len(even)
    size, depth = odd[0].shape
    wide = factor.shape[1]
    return pl.pallas_call(
        lambda *refs: early_kernel(n, m, *refs),
        out_shape=(
            jax.ShapeDtypeStruct((size, wide // 2), BF16),
            jax.ShapeDtypeStruct((size, wide // 2), F32),
            jax.ShapeDtypeStruct((size, wide), F32),
        ),
        in_specs=[pl.BlockSpec(memory_space=pltpu.SMEM)] + [pl.BlockSpec(memory_space=pl.ANY)] * (n + m + 1),
        out_specs=(pl.BlockSpec(memory_space=pltpu.VMEM),) * 3,
        scratch_shapes=[
            pltpu.VMEM((n + m, size, depth), BF16),
            pltpu.VMEM(factor.shape, BF16),
            pltpu.VMEM((size, wide), F32),
            pltpu.SemaphoreType.DMA((2 * (n + m),)),
        ],
        compiler_params=pltpu.CompilerParams(vmem_limit_bytes=56 * 2**20),
        cost_estimate=pl.CostEstimate(
            flops=2 * (n + m) * size * depth * wide, bytes_accessed=12 * 2**20, transcendentals=0
        ),
    )(jnp.stack(at).astype(jnp.int32), *odd, *even, factor)


def body(weight, anchor, input_factor, output_factor, task_grad):
    y, xh, xl, z, core = (lax.axis_index(a) for a in ROW + COL)
    change = (weight.astype(F32) - anchor.astype(F32)).astype(BF16)
    rows, cols = weight.shape
    half = rows // 2

    depth = input_factor.shape[0] // 2
    mine = lax.dynamic_slice_in_dim(input_factor, core * depth, depth, 0)
    other = lax.dynamic_slice_in_dim(input_factor, (1 - core) * depth, depth, 0)
    pair = jnp.concatenate([mine, shift(other, "core", 1)], axis=1)
    factor = lax.all_gather(pair, "y", axis=0, tiled=True)

    b = turn(change)
    bm, bp, a = together(shift(b, "z", 1), shift(b, "z", -1), shift(b, "xl", 1))
    am, ap, b2 = together(shift(bm, "xl", 1), shift(a, "z", -1), shift(bm, "z", 1))
    turned = turn(after(output_factor, bm, bp, a))
    far = [shift(am[:half], "z", 1), shift(ap[half:], "z", -1)]
    *far, part = together(*far, shift(after(turned, factor), "xl", 1))

    def place(dxl, dz):
        return (xl ^ dxl) * 2 + (((z + dz) & 3) >> 1)

    at = [place(0, -1), place(0, 1), place(1, -1), place(1, 1), place(0, 0), place(1, 0), place(1, 2)]
    theirs, own, even = early([am, ap, bm, bp], [a, b, b2], factor, at)
    part = jnp.concatenate([after(part, own), turned], axis=0)
    left = lax.all_gather(part, ("core", "z"), axis=0)

    def more(side):
        right = lax.dynamic_slice(factor, (place(0, 2) * depth, side * cols), (depth, cols))
        last = jnp.concatenate([dot(v, right) for v in far], axis=0)
        return even[:, side * cols : (side + 1) * cols] + last

    theirs = [after(theirs, more(1)), more(1).astype(BF16)]
    odd, even = [v + shift(w, "core", 1).astype(F32) for v, w in zip((own, more(0)), theirs)]
    same = (z & 1) == xh
    send, keep = jnp.where(same, odd, even).astype(BF16), jnp.where(same, even, odd)
    send = shift(send, "xh", 1)

    p = [(keep[r] + send[r].astype(F32)).astype(BF16) for r in (slice(half), slice(half, rows))]
    below = [shift(p[0], "y", 1), shift(p[1], "y", 1)]
    above = [shift(p[0], "y", -1), shift(p[1], "y", -1)]
    beyond = [shift(below[0], "y", 1), shift(above[1], "y", -1)]

    def share(blocks, dy):
        at = (y + dy) & 3
        size = (2, rows, half)
        corners = [(4 * h + (at & 1) * 2, ((at >> 1) ^ xl) * rows, 0) for h in range(2)]
        terms = [dot(lax.dynamic_slice(left, c, size), v) for c, v in zip(corners, blocks)]
        return terms[0] + terms[1]

    penalty = ((share(p, 0) + share(below, -1)) + share(above, 1)) + share(beyond, 2)
    penalty = penalty.astype(BF16).reshape(2 * rows, cols)
    owned = lax.all_to_all(penalty, ("xh",) + COL, split_axis=0, concat_axis=0, tiled=True)
    owned = owned.reshape(2, 16, task_grad.shape[0], cols).astype(F32).sum(axis=0)
    owned = owned.transpose(1, 0, 2).reshape(task_grad.shape)
    return (task_grad.astype(F32) + owned).astype(BF16)


def solution(mesh):
    fine = Mesh(mesh.devices.reshape(4, 2, 2, 4, 2), ROW + COL)
    cut = P(ROW, COL)
    placed = (cut, cut, cut, cut, P(ROW + COL, None))
    return jax.shard_map(
        body, mesh=fine, in_specs=placed, out_specs=P(ROW + COL, None), check_vma=False
    )
```

```python
import jax
import jax.numpy as jnp
from jax import lax
from jax.experimental import pallas as pl
from jax.experimental.pallas import tpu as pltpu
from jax.sharding import Mesh, PartitionSpec as P

ROW = ("y", "xh")
COL = ("xl", "z", "core")
F32, BF16 = jnp.float32, jnp.bfloat16


def shift(v, axis, by):
    n = lax.axis_size(axis)
    return lax.ppermute(v, axis, [(i, (i + by) % n) for i in range(n)])


def turn(v, flip=True):
    pairs = []
    for xh in range(2):
        for xl in range(2):
            for z in range(4):
                new_xl = 1 - xl if flip or z & 1 != xh else xl
                to = ((z & 1) * 2 + new_xl) * 4 + (z & ~1) + xh
                pairs.append(((xh * 2 + xl) * 4 + z, to))
    return lax.ppermute(v, ("xh", "xl", "z"), pairs)


def after(v, *done):
    return lax.optimization_barrier((v, *done))[0]


def together(*arrays):
    return lax.optimization_barrier(arrays)


def dot(a, b):
    return lax.dot_general(a, b, (((a.ndim - 1,), (0,)), ((), ())), preferred_element_type=F32)


def early_kernel(n, m, at, *refs):
    blocks, factor = refs[: n + m], refs[n + m]
    theirs, own, part, held, right, total, came = refs[n + m + 1 :]
    size, depth = blocks[0].shape
    cols = own.shape[1]
    rows = [pl.ds(pl.multiple_of(at[i] * depth, depth), depth) for i in range(n + m)]
    copies = []
    for i in range(n + m):
        copies.append([pltpu.make_async_copy(blocks[i], held.at[i], came.at[2 * i])])
        if i < n:
            copies[i].append(pltpu.make_async_copy(factor.at[rows[i]], right.at[rows[i]], came.at[2 * i + 1]))
    for copy in sum(copies, []):
        copy.start()
    step = min(256, cols)
    for lo, hi in ((0, n // 2), (n // 2, n), (n, n + m)):
        for copy in sum(copies[lo:hi], []):
            copy.wait()
        for c in range(0, 2 * cols, step):
            here = slice(c, c + step)
            value = None
            for i in range(lo, hi):
                more = dot(held[i], right[rows[i], here])
                value = more if value is None else value + more
            if lo == 0:
                total[:, here] = value
            elif hi > n:
                part[:, here] = value
            elif c < cols:
                own[:, here] = total[:, here] + value
            else:
                theirs[:, c - cols : c - cols + step] = (total[:, here] + value).astype(BF16)


def early(odd, even, factor, at):
    n, m = len(odd), len(even)
    size, depth = odd[0].shape
    wide = factor.shape[1]
    return pl.pallas_call(
        lambda *refs: early_kernel(n, m, *refs),
        out_shape=(
            jax.ShapeDtypeStruct((size, wide // 2), BF16),
            jax.ShapeDtypeStruct((size, wide // 2), F32),
            jax.ShapeDtypeStruct((size, wide), F32),
        ),
        in_specs=[pl.BlockSpec(memory_space=pltpu.SMEM)] + [pl.BlockSpec(memory_space=pl.ANY)] * (n + m + 1),
        out_specs=(pl.BlockSpec(memory_space=pltpu.VMEM),) * 3,
        scratch_shapes=[
            pltpu.VMEM((n + m, size, depth), BF16),
            pltpu.VMEM(factor.shape, BF16),
            pltpu.VMEM((size, wide), F32),
            pltpu.SemaphoreType.DMA((2 * (n + m),)),
        ],
        compiler_params=pltpu.CompilerParams(vmem_limit_bytes=56 * 2**20),
        cost_estimate=pl.CostEstimate(
            flops=2 * (n + m) * size * depth * wide, bytes_accessed=12 * 2**20, transcendentals=0
        ),
    )(jnp.stack(at).astype(jnp.int32), *odd, *even, factor)


def body(weight, anchor, input_factor, output_factor, task_grad):
    y, xh, xl, z, core = (lax.axis_index(a) for a in ROW + COL)
    change = (weight.astype(F32) - anchor.astype(F32)).astype(BF16)
    rows, cols = weight.shape
    half = rows // 2

    depth = input_factor.shape[0] // 2
    mine = lax.dynamic_slice_in_dim(input_factor, core * depth, depth, 0)
    other = lax.dynamic_slice_in_dim(input_factor, (1 - core) * depth, depth, 0)
    pair = jnp.concatenate([mine, shift(other, "core", 1)], axis=1)
    factor = lax.all_gather(pair, "y", axis=0, tiled=True)

    b = turn(change)
    bm, bp, a = together(shift(b, "z", 1), shift(b, "z", -1), shift(b, "xl", 1))
    am, ap, b2 = together(shift(bm, "xl", 1), shift(a, "z", -1), shift(bm, "z", 1))
    turned = turn(after(output_factor, bm, bp, a), flip=False)
    far = [shift(am[:half], "z", 1), shift(ap[half:], "z", -1)]
    *far, part = together(*far, shift(after(turned, factor), "xl", 1))

    def place(dxl, dz):
        return (xl ^ dxl) * 2 + (((z + dz) & 3) >> 1)

    at = [place(0, -1), place(0, 1), place(1, -1), place(1, 1), place(0, 0), place(1, 0), place(1, 2)]
    theirs, own, even = early([am, ap, bm, bp], [a, b, b2], factor, at)
    part = jnp.concatenate([after(part, own), turned], axis=0)
    left = lax.all_gather(part, ("core", "z"), axis=0)

    def more(side):
        right = lax.dynamic_slice(factor, (place(0, 2) * depth, side * cols), (depth, cols))
        last = jnp.concatenate([dot(v, right) for v in far], axis=0)
        return even[:, side * cols : (side + 1) * cols] + last

    theirs = [after(theirs, more(1)), more(1).astype(BF16)]
    odd, even = [v + shift(w, "core", 1).astype(F32) for v, w in zip((own, more(0)), theirs)]
    same = (z & 1) == xh
    send, keep = jnp.where(same, odd, even).astype(BF16), jnp.where(same, even, odd)
    send = shift(send, "xh", 1)

    p = [(keep[r] + send[r].astype(F32)).astype(BF16) for r in (slice(half), slice(half, rows))]
    below = [shift(p[0], "y", 1), shift(p[1], "y", 1)]
    above = [shift(p[0], "y", -1), shift(p[1], "y", -1)]
    beyond = [shift(below[0], "y", 1), shift(above[1], "y", -1)]

    def share(blocks, dy, to):
        at = (y + dy) & 3
        here = 1 - ((at >> 1) ^ xl ^ to ^ xh)
        corners = [(4 * h + (at & 1) * 2 + to, here * rows, 0) for h in range(2)]
        sides = [lax.dynamic_slice(left, c, (1, rows, half))[0] for c in corners]
        return dot(sides[0], blocks[0]) + dot(sides[1], blocks[1])

    penalty = [
        ((share(p, 0, to) + share(below, -1, to)) + share(above, 1, to)) + share(beyond, 2, to)
        for to in range(2)
    ]
    penalty = jnp.stack(penalty)
    penalty = penalty.astype(BF16).reshape(2 * rows, cols)
    owned = lax.all_to_all(penalty, ("xh",) + COL, split_axis=0, concat_axis=0, tiled=True)
    owned = owned.reshape(2, 16, task_grad.shape[0], cols).astype(F32).sum(axis=0)
    owned = owned.transpose(1, 0, 2).reshape(task_grad.shape)
    return (task_grad.astype(F32) + owned).astype(BF16)


def solution(mesh):
    fine = Mesh(mesh.devices.reshape(4, 2, 2, 4, 2), ROW + COL)
    cut = P(ROW, COL)
    placed = (cut, cut, cut, cut, P(ROW + COL, None))
    return jax.shard_map(
        body, mesh=fine, in_specs=placed, out_specs=P(ROW + COL, None), check_vma=False
    )
```

```python
import jax
import jax.numpy as jnp
from jax import lax
from jax.experimental import pallas as pl
from jax.experimental.pallas import tpu as pltpu
from jax.sharding import Mesh, PartitionSpec as P

ROW = ("y", "xh")
COL = ("xl", "z", "core")
F32, BF16 = jnp.float32, jnp.bfloat16


def shift(v, axis, by):
    n = lax.axis_size(axis)
    return lax.ppermute(v, axis, [(i, (i + by) % n) for i in range(n)])


def turn(v):
    pairs = []
    for xh in range(2):
        for xl in range(2):
            for z in range(4):
                to = ((z & 1) * 2 + 1 - xl) * 4 + (z & ~1) + xh
                pairs.append(((xh * 2 + xl) * 4 + z, to))
    return lax.ppermute(v, ("xh", "xl", "z"), pairs)


def part_ways(v, where, to):
    every = [(xh, xl, z) for xh in range(2) for xl in range(2) for z in range(4)]
    pairs = [(p, to(*p)) for p in every if where(*p)]
    return lax.ppermute(v, ("xh", "xl", "z"), [tuple((q[0] * 2 + q[1]) * 4 + q[2] for q in pair) for pair in pairs])


def after(v, *done):
    return lax.optimization_barrier((v, *done))[0]


def together(*arrays):
    return lax.optimization_barrier(arrays)


def dot(a, b):
    return lax.dot_general(a, b, (((a.ndim - 1,), (0,)), ((), ())), preferred_element_type=F32)


def early_kernel(n, m, at, *refs):
    blocks, factor = refs[: n + m], refs[n + m]
    theirs, own, part, held, right, total, came = refs[n + m + 1 :]
    size, depth = blocks[0].shape
    cols = own.shape[1]
    rows = [pl.ds(pl.multiple_of(at[i] * depth, depth), depth) for i in range(n + m)]
    copies = []
    for i in range(n + m):
        copies.append([pltpu.make_async_copy(blocks[i], held.at[i], came.at[2 * i])])
        if i < n:
            copies[i].append(pltpu.make_async_copy(factor.at[rows[i]], right.at[rows[i]], came.at[2 * i + 1]))
    for copy in sum(copies, []):
        copy.start()
    step = min(256, cols)
    for lo, hi in ((0, n // 2), (n // 2, n), (n, n + m)):
        for copy in sum(copies[lo:hi], []):
            copy.wait()
        for c in range(0, 2 * cols, step):
            here = slice(c, c + step)
            value = None
            for i in range(lo, hi):
                more = dot(held[i], right[rows[i], here])
                value = more if value is None else value + more
            if lo == 0:
                total[:, here] = value
            elif hi > n:
                part[:, here] = value
            elif c < cols:
                own[:, here] = total[:, here] + value
            else:
                theirs[:, c - cols : c - cols + step] = (total[:, here] + value).astype(BF16)


def early(odd, even, factor, at):
    n, m = len(odd), len(even)
    size, depth = odd[0].shape
    wide = factor.shape[1]
    return pl.pallas_call(
        lambda *refs: early_kernel(n, m, *refs),
        out_shape=(
            jax.ShapeDtypeStruct((size, wide // 2), BF16),
            jax.ShapeDtypeStruct((size, wide // 2), F32),
            jax.ShapeDtypeStruct((size, wide), F32),
        ),
        in_specs=[pl.BlockSpec(memory_space=pltpu.SMEM)] + [pl.BlockSpec(memory_space=pl.ANY)] * (n + m + 1),
        out_specs=(pl.BlockSpec(memory_space=pltpu.VMEM),) * 3,
        scratch_shapes=[
            pltpu.VMEM((n + m, size, depth), BF16),
            pltpu.VMEM(factor.shape, BF16),
            pltpu.VMEM((size, wide), F32),
            pltpu.SemaphoreType.DMA((2 * (n + m),)),
        ],
        compiler_params=pltpu.CompilerParams(vmem_limit_bytes=56 * 2**20),
        cost_estimate=pl.CostEstimate(
            flops=2 * (n + m) * size * depth * wide, bytes_accessed=12 * 2**20, transcendentals=0
        ),
    )(jnp.stack(at).astype(jnp.int32), *odd, *even, factor)


def body(weight, anchor, input_factor, output_factor, task_grad):
    y, xh, xl, z, core = (lax.axis_index(a) for a in ROW + COL)
    change = (weight.astype(F32) - anchor.astype(F32)).astype(BF16)
    rows, cols = weight.shape
    half = rows // 2

    depth = input_factor.shape[0] // 2
    mine = lax.dynamic_slice_in_dim(input_factor, core * depth, depth, 0)
    other = lax.dynamic_slice_in_dim(input_factor, (1 - core) * depth, depth, 0)
    pair = jnp.concatenate([mine, shift(other, "core", 1)], axis=1)
    factor = lax.all_gather(pair, "y", axis=0, tiled=True)

    moves = part_ways(output_factor, lambda xh, xl, z: z & 1 != xh, lambda xh, xl, z: (xh, xl, (z + 2 * (z & 1) - 1) & 3))
    b, moves = together(turn(change), moves)
    moves = part_ways(moves, lambda xh, xl, z: z & 1 == xh, lambda xh, xl, z: (1 - xh, 1 - xl, z))
    bm, bp, a, moves = together(shift(b, "z", 1), shift(b, "z", -1), shift(b, "xl", 1), moves)
    am, ap, b2 = together(shift(bm, "xl", 1), shift(a, "z", -1), shift(bm, "z", 1))
    same = (z & 1) == xh
    turned = jnp.where(same, output_factor, moves)
    far = [shift(am[:half], "z", 1), shift(ap[half:], "z", -1)]
    *far, part = together(*far, shift(after(turned, factor), "xl", 1))

    def place(dxl, dz):
        return (xl ^ dxl) * 2 + (((z + dz) & 3) >> 1)

    at = [place(0, -1), place(0, 1), place(1, -1), place(1, 1), place(0, 0), place(1, 0), place(1, 2)]
    theirs, own, even = early([am, ap, bm, bp], [a, b, b2], factor, at)
    part = jnp.concatenate([after(part, own), turned], axis=0)
    left = lax.all_gather(part, ("core", "z"), axis=0)

    def more(side):
        right = lax.dynamic_slice(factor, (place(0, 2) * depth, side * cols), (depth, cols))
        last = jnp.concatenate([dot(v, right) for v in far], axis=0)
        return even[:, side * cols : (side + 1) * cols] + last

    theirs = [after(theirs, more(1)), more(1).astype(BF16)]
    odd, even = [v + shift(w, "core", 1).astype(F32) for v, w in zip((own, more(0)), theirs)]
    send, keep = jnp.where(same, odd, even).astype(BF16), jnp.where(same, even, odd)
    send = shift(send, "xh", 1)

    p = [(keep[r] + send[r].astype(F32)).astype(BF16) for r in (slice(half), slice(half, rows))]
    below = [shift(p[0], "y", 1), shift(p[1], "y", 1)]
    above = [shift(p[0], "y", -1), shift(p[1], "y", -1)]
    beyond = [shift(below[0], "y", 1), shift(above[1], "y", -1)]

    def share(blocks, dy, to):
        at = ((y + dy) & 3) ^ (3 * (to ^ xh))
        here = 1 - ((at >> 1) ^ xl)
        corners = [(4 * h + (at & 1) * 2 + to, here * rows, 0) for h in range(2)]
        sides = [lax.dynamic_slice(left, c, (1, rows, half))[0] for c in corners]
        return dot(sides[0], blocks[0]) + dot(sides[1], blocks[1])

    penalty = [
        ((share(p, 0, to) + share(below, -1, to)) + share(above, 1, to)) + share(beyond, 2, to)
        for to in range(2)
    ]
    penalty = jnp.stack(penalty)
    penalty = penalty.astype(BF16).reshape(2 * rows, cols)
    owned = lax.all_to_all(penalty, ("xh",) + COL, split_axis=0, concat_axis=0, tiled=True)
    owned = owned.reshape(2, 16, task_grad.shape[0], cols).astype(F32).sum(axis=0)
    owned = owned.transpose(1, 0, 2).reshape(task_grad.shape)
    return (task_grad.astype(F32) + owned).astype(BF16)


def solution(mesh):
    fine = Mesh(mesh.devices.reshape(4, 2, 2, 4, 2), ROW + COL)
    cut = P(ROW, COL)
    placed = (cut, cut, cut, cut, P(ROW + COL, None))
    return jax.shard_map(
        body, mesh=fine, in_specs=placed, out_specs=P(ROW + COL, None), check_vma=False
    )
```

```python
import jax
import jax.numpy as jnp
from jax import lax
from jax.experimental import pallas as pl
from jax.experimental.pallas import tpu as pltpu
from jax.sharding import Mesh, PartitionSpec as P

ROW = ("y", "xh")
COL = ("xl", "z", "core")
F32, BF16 = jnp.float32, jnp.bfloat16


def shift(v, axis, by):
    n = lax.axis_size(axis)
    return lax.ppermute(v, axis, [(i, (i + by) % n) for i in range(n)])


def turn(v):
    pairs = []
    for xh in range(2):
        for xl in range(2):
            for z in range(4):
                to = ((z & 1) * 2 + 1 - xl) * 4 + (z & ~1) + xh
                pairs.append(((xh * 2 + xl) * 4 + z, to))
    return lax.ppermute(v, ("xh", "xl", "z"), pairs)


def part_ways(v, where, to):
    every = [(xh, xl, z) for xh in range(2) for xl in range(2) for z in range(4)]
    pairs = [(p, to(*p)) for p in every if where(*p)]
    return lax.ppermute(v, ("xh", "xl", "z"), [tuple((q[0] * 2 + q[1]) * 4 + q[2] for q in pair) for pair in pairs])


def after(v, *done):
    return lax.optimization_barrier((v, *done))[0]


def together(*arrays):
    return lax.optimization_barrier(arrays)


def dot(a, b):
    return lax.dot_general(a, b, (((a.ndim - 1,), (0,)), ((), ())), preferred_element_type=F32)


def early_kernel(n, m, at, *refs):
    blocks, factor = refs[: n + m], refs[n + m]
    theirs, own, part, held, right, total, came = refs[n + m + 1 :]
    size, depth = blocks[0].shape
    cols = own.shape[1]
    rows = [pl.ds(pl.multiple_of(at[i] * depth, depth), depth) for i in range(n + m)]
    copies = []
    for i in range(n + m):
        copies.append([pltpu.make_async_copy(blocks[i], held.at[i], came.at[2 * i])])
        if i < n:
            copies[i].append(pltpu.make_async_copy(factor.at[rows[i]], right.at[rows[i]], came.at[2 * i + 1]))
    for copy in sum(copies, []):
        copy.start()
    step = min(256, cols)
    for lo, hi in ((0, n // 2), (n // 2, n), (n, n + m)):
        for copy in sum(copies[lo:hi], []):
            copy.wait()
        for c in range(0, 2 * cols, step):
            here = slice(c, c + step)
            value = None
            for i in range(lo, hi):
                more = dot(held[i], right[rows[i], here])
                value = more if value is None else value + more
            if lo == 0:
                total[:, here] = value
            elif hi > n:
                part[:, here] = value
            elif c < cols:
                own[:, here] = total[:, here] + value
            else:
                theirs[:, c - cols : c - cols + step] = (total[:, here] + value).astype(BF16)


def early(odd, even, factor, at):
    n, m = len(odd), len(even)
    size, depth = odd[0].shape
    wide = factor.shape[1]
    return pl.pallas_call(
        lambda *refs: early_kernel(n, m, *refs),
        out_shape=(
            jax.ShapeDtypeStruct((size, wide // 2), BF16),
            jax.ShapeDtypeStruct((size, wide // 2), F32),
            jax.ShapeDtypeStruct((size, wide), F32),
        ),
        in_specs=[pl.BlockSpec(memory_space=pltpu.SMEM)] + [pl.BlockSpec(memory_space=pl.ANY)] * (n + m + 1),
        out_specs=(pl.BlockSpec(memory_space=pltpu.VMEM),) * 3,
        scratch_shapes=[
            pltpu.VMEM((n + m, size, depth), BF16),
            pltpu.VMEM(factor.shape, BF16),
            pltpu.VMEM((size, wide), F32),
            pltpu.SemaphoreType.DMA((2 * (n + m),)),
        ],
        compiler_params=pltpu.CompilerParams(vmem_limit_bytes=56 * 2**20),
        cost_estimate=pl.CostEstimate(
            flops=2 * (n + m) * size * depth * wide, bytes_accessed=12 * 2**20, transcendentals=0
        ),
    )(jnp.stack(at).astype(jnp.int32), *odd, *even, factor)


def body(weight, anchor, input_factor, output_factor, task_grad):
    y, xh, xl, z, core = (lax.axis_index(a) for a in ROW + COL)
    change = (weight.astype(F32) - anchor.astype(F32)).astype(BF16)
    rows, cols = weight.shape
    half = rows // 2

    depth = input_factor.shape[0] // 2
    mine = lax.dynamic_slice_in_dim(input_factor, core * depth, depth, 0)
    other = lax.dynamic_slice_in_dim(input_factor, (1 - core) * depth, depth, 0)
    pair = jnp.concatenate([mine, shift(other, "core", 1)], axis=1)
    factor = lax.all_gather(pair, "y", axis=0, tiled=True)

    moves = part_ways(output_factor, lambda xh, xl, z: z & 1 != xh, lambda xh, xl, z: (xh, 1 - xl, z ^ 1))
    b, moves = together(turn(change), moves)
    moves = part_ways(moves, lambda xh, xl, z: z & 1 == xh, lambda xh, xl, z: (1 - xh, 1 - xl, z))
    bm, bp, a, moves = together(shift(b, "z", 1), shift(b, "z", -1), shift(b, "xl", 1), moves)
    am, ap, b2 = together(shift(bm, "xl", 1), shift(a, "z", -1), shift(bm, "z", 1))
    same = (z & 1) == xh
    turned = jnp.where(same, output_factor, moves)
    far = [shift(am[:half], "z", 1), shift(ap[half:], "z", -1)]
    *far, part = together(*far, shift(after(turned, factor), "xl", 1))

    def place(dxl, dz):
        return (xl ^ dxl) * 2 + (((z + dz) & 3) >> 1)

    at = [place(0, -1), place(0, 1), place(1, -1), place(1, 1), place(0, 0), place(1, 0), place(1, 2)]
    theirs, own, even = early([am, ap, bm, bp], [a, b, b2], factor, at)
    part = jnp.concatenate([after(part, own), turned], axis=0)
    left = lax.all_gather(part, ("core", "z"), axis=0)

    def more(side):
        right = lax.dynamic_slice(factor, (place(0, 2) * depth, side * cols), (depth, cols))
        last = jnp.concatenate([dot(v, right) for v in far], axis=0)
        return even[:, side * cols : (side + 1) * cols] + last

    theirs = [after(theirs, more(1)), more(1).astype(BF16)]
    odd, even = [v + shift(w, "core", 1).astype(F32) for v, w in zip((own, more(0)), theirs)]
    top, rest = slice(half), slice(half, rows)
    first, second = [jnp.where(same, odd[r], even[r]).astype(BF16) for r in (top, rest)]
    first = shift(first, "xh", 1)
    second = shift(after(second, first), "xh", 1)
    keep = jnp.where(same, even, odd)

    p = [(keep[top] + first.astype(F32)).astype(BF16)]
    below, above = [shift(p[0], "y", 1)], [shift(p[0], "y", -1)]
    second, above[0] = together(second, above[0])
    p.append((keep[rest] + second.astype(F32)).astype(BF16))
    below.append(shift(p[1], "y", 1))
    above.append(shift(p[1], "y", -1))
    beyond = [shift(below[0], "y", 1), shift(above[1], "y", -1)]

    def share(blocks, dy):
        at = (y + dy) & 3
        size = (2, rows, half)
        corners = [(4 * h + (at & 1) * 2, (1 ^ (at >> 1) ^ xl) * rows, 0) for h in range(2)]
        terms = [dot(lax.dynamic_slice(left, c, size), v) for c, v in zip(corners, blocks)]
        return terms[0] + terms[1]

    penalty = ((share(p, 0) + share(below, -1)) + share(above, 1)) + share(beyond, 2)
    penalty = penalty.astype(BF16).reshape(2 * rows, cols)
    owned = lax.all_to_all(penalty, ("xh",) + COL, split_axis=0, concat_axis=0, tiled=True)
    owned = owned.reshape(2, 16, task_grad.shape[0], cols).astype(F32).sum(axis=0)
    owned = owned.transpose(1, 0, 2).reshape(task_grad.shape)
    return (task_grad.astype(F32) + owned).astype(BF16)


def solution(mesh):
    fine = Mesh(mesh.devices.reshape(4, 2, 2, 4, 2), ROW + COL)
    cut = P(ROW, COL)
    placed = (cut, cut, cut, cut, P(ROW + COL, None))
    return jax.shard_map(
        body, mesh=fine, in_specs=placed, out_specs=P(ROW + COL, None), check_vma=False
    )
```

```python
import jax
import jax.numpy as jnp
from jax import lax
from jax.experimental import pallas as pl
from jax.experimental.pallas import tpu as pltpu
from jax.sharding import Mesh, PartitionSpec as P

ROW = ("y", "xh")
COL = ("xl", "z", "core")
F32, BF16 = jnp.float32, jnp.bfloat16


def shift(v, axis, by):
    n = lax.axis_size(axis)
    return lax.ppermute(v, axis, [(i, (i + by) % n) for i in range(n)])


def turn(v):
    pairs = []
    for xh in range(2):
        for xl in range(2):
            for z in range(4):
                to = ((z & 1) * 2 + 1 - xl) * 4 + (z & ~1) + xh
                pairs.append(((xh * 2 + xl) * 4 + z, to))
    return lax.ppermute(v, ("xh", "xl", "z"), pairs)


def part_ways(v, where, to):
    every = [(xh, xl, z) for xh in range(2) for xl in range(2) for z in range(4)]
    pairs = [(p, to(*p)) for p in every if where(*p)]
    return lax.ppermute(v, ("xh", "xl", "z"), [tuple((q[0] * 2 + q[1]) * 4 + q[2] for q in pair) for pair in pairs])


def after(v, *done):
    return lax.optimization_barrier((v, *done))[0]


def together(*arrays):
    return lax.optimization_barrier(arrays)


def dot(a, b):
    return lax.dot_general(a, b, (((a.ndim - 1,), (0,)), ((), ())), preferred_element_type=F32)


def early_kernel(n, m, at, *refs):
    blocks, factor = refs[: n + m], refs[n + m]
    theirs, own, part, held, right, total, came = refs[n + m + 1 :]
    size, depth = blocks[0].shape
    cols = own.shape[1]
    rows = [pl.ds(pl.multiple_of(at[i] * depth, depth), depth) for i in range(n + m)]
    copies = []
    for i in range(n + m):
        copies.append([pltpu.make_async_copy(blocks[i], held.at[i], came.at[2 * i])])
        if i < n:
            copies[i].append(pltpu.make_async_copy(factor.at[rows[i]], right.at[rows[i]], came.at[2 * i + 1]))
    for copy in sum(copies, []):
        copy.start()
    step = min(256, cols)
    for lo, hi in ((0, n // 2), (n // 2, n), (n, n + m)):
        for copy in sum(copies[lo:hi], []):
            copy.wait()
        for c in range(0, 2 * cols, step):
            here = slice(c, c + step)
            value = None
            for i in range(lo, hi):
                more = dot(held[i], right[rows[i], here])
                value = more if value is None else value + more
            if lo == 0:
                total[:, here] = value
            elif hi > n:
                part[:, here] = value
            elif c < cols:
                own[:, here] = total[:, here] + value
            else:
                theirs[:, c - cols : c - cols + step] = (total[:, here] + value).astype(BF16)


def early(odd, even, factor, at):
    n, m = len(odd), len(even)
    size, depth = odd[0].shape
    wide = factor.shape[1]
    return pl.pallas_call(
        lambda *refs: early_kernel(n, m, *refs),
        out_shape=(
            jax.ShapeDtypeStruct((size, wide // 2), BF16),
            jax.ShapeDtypeStruct((size, wide // 2), F32),
            jax.ShapeDtypeStruct((size, wide), F32),
        ),
        in_specs=[pl.BlockSpec(memory_space=pltpu.SMEM)] + [pl.BlockSpec(memory_space=pl.ANY)] * (n + m + 1),
        out_specs=(pl.BlockSpec(memory_space=pltpu.VMEM),) * 3,
        scratch_shapes=[
            pltpu.VMEM((n + m, size, depth), BF16),
            pltpu.VMEM(factor.shape, BF16),
            pltpu.VMEM((size, wide), F32),
            pltpu.SemaphoreType.DMA((2 * (n + m),)),
        ],
        compiler_params=pltpu.CompilerParams(vmem_limit_bytes=56 * 2**20),
        cost_estimate=pl.CostEstimate(
            flops=2 * (n + m) * size * depth * wide, bytes_accessed=12 * 2**20, transcendentals=0
        ),
    )(jnp.stack(at).astype(jnp.int32), *odd, *even, factor)


def body(weight, anchor, input_factor, output_factor, task_grad):
    y, xh, xl, z, core = (lax.axis_index(a) for a in ROW + COL)
    change = (weight.astype(F32) - anchor.astype(F32)).astype(BF16)
    rows, cols = weight.shape
    half = rows // 2

    depth = input_factor.shape[0] // 2
    mine = lax.dynamic_slice_in_dim(input_factor, core * depth, depth, 0)
    other = lax.dynamic_slice_in_dim(input_factor, (1 - core) * depth, depth, 0)
    pair = jnp.concatenate([mine, shift(other, "core", 1)], axis=1)
    factor = lax.all_gather(pair, "y", axis=0, tiled=True)

    moves = part_ways(output_factor, lambda xh, xl, z: z & 1 != xh, lambda xh, xl, z: (xh, 1 - xl, z ^ 1))
    b, moves = together(turn(change), moves)
    moves = part_ways(moves, lambda xh, xl, z: z & 1 == xh, lambda xh, xl, z: (1 - xh, 1 - xl, z))
    bm, bp, a, moves = together(shift(b, "z", 1), shift(b, "z", -1), shift(b, "xl", 1), moves)
    am, ap, b2 = together(shift(bm, "xl", 1), shift(a, "z", -1), shift(bm, "z", 1))
    same = (z & 1) == xh
    turned = jnp.where(same, output_factor, moves)
    far = [shift(am[:half], "z", 1), shift(ap[half:], "z", -1)]
    *far, part = together(*far, shift(after(turned, factor), "xl", 1))

    def place(dxl, dz):
        return (xl ^ dxl) * 2 + (((z + dz) & 3) >> 1)

    at = [place(0, -1), place(0, 1), place(1, -1), place(1, 1), place(0, 0), place(1, 0), place(1, 2)]
    theirs, own, even = early([am, ap, bm, bp], [a, b, b2], factor, at)
    part = jnp.concatenate([after(part, own), turned], axis=0)
    left = lax.all_gather(part, ("core", "z"), axis=0)

    def more(side):
        right = lax.dynamic_slice(factor, (place(0, 2) * depth, side * cols), (depth, cols))
        last = jnp.concatenate([dot(v, right) for v in far], axis=0)
        return even[:, side * cols : (side + 1) * cols] + last

    theirs = [after(theirs, more(1)), more(1).astype(BF16)]
    odd, even = [v + shift(w, "core", 1).astype(F32) for v, w in zip((own, more(0)), theirs)]
    top, rest = slice(half), slice(half, rows)
    first, second = [jnp.where(same, odd[r], even[r]).astype(BF16) for r in (top, rest)]
    first = shift(first, "xh", 1)
    second = shift(after(second, first), "xh", 1)
    keep = jnp.where(same, even, odd)

    grad, first = together(task_grad.astype(F32), first)
    p = [(keep[top] + first.astype(F32)).astype(BF16)]
    below, above = [shift(p[0], "y", 1)], [shift(p[0], "y", -1)]
    second, above[0] = together(second, above[0])
    p.append((keep[rest] + second.astype(F32)).astype(BF16))
    below.append(shift(p[1], "y", 1))
    above.append(shift(p[1], "y", -1))
    beyond = [shift(below[0], "y", 1), shift(above[1], "y", -1)]

    def share(blocks, dy):
        at = (y + dy) & 3
        size = (2, rows, half)
        corners = [(4 * h + (at & 1) * 2, (1 ^ (at >> 1) ^ xl) * rows, 0) for h in range(2)]
        terms = [dot(lax.dynamic_slice(left, c, size), v) for c, v in zip(corners, blocks)]
        return terms[0] + terms[1]

    penalty = ((share(p, 0) + share(below, -1)) + share(above, 1)) + share(beyond, 2)
    penalty = penalty.astype(BF16).reshape(2 * rows, cols)
    owned = lax.all_to_all(penalty, ("xh",) + COL, split_axis=0, concat_axis=0, tiled=True)
    owned = owned.reshape(2, 16, task_grad.shape[0], cols).astype(F32).sum(axis=0)
    owned = owned.transpose(1, 0, 2).reshape(task_grad.shape)
    return (grad + owned).astype(BF16)


def solution(mesh):
    fine = Mesh(mesh.devices.reshape(4, 2, 2, 4, 2), ROW + COL)
    cut = P(ROW, COL)
    placed = (cut, cut, cut, cut, P(ROW + COL, None))
    return jax.shard_map(
        body, mesh=fine, in_specs=placed, out_specs=P(ROW + COL, None), check_vma=False
    )
```

```python
import jax
import jax.numpy as jnp
from jax import lax
from jax.experimental import pallas as pl
from jax.experimental.pallas import tpu as pltpu
from jax.sharding import Mesh, PartitionSpec as P

ROW = ("y", "xh")
COL = ("xl", "z", "core")
F32, BF16 = jnp.float32, jnp.bfloat16


def shift(v, axis, by):
    n = lax.axis_size(axis)
    return lax.ppermute(v, axis, [(i, (i + by) % n) for i in range(n)])


def turn(v):
    pairs = []
    for xh in range(2):
        for xl in range(2):
            for z in range(4):
                to = ((z & 1) * 2 + 1 - xl) * 4 + (z & ~1) + xh
                pairs.append(((xh * 2 + xl) * 4 + z, to))
    return lax.ppermute(v, ("xh", "xl", "z"), pairs)


def part_ways(v, where, to):
    every = [(xh, xl, z) for xh in range(2) for xl in range(2) for z in range(4)]
    pairs = [(p, to(*p)) for p in every if where(*p)]
    return lax.ppermute(v, ("xh", "xl", "z"), [tuple((q[0] * 2 + q[1]) * 4 + q[2] for q in pair) for pair in pairs])


def after(v, *done):
    return lax.optimization_barrier((v, *done))[0]


def together(*arrays):
    return lax.optimization_barrier(arrays)


def dot(a, b):
    return lax.dot_general(a, b, (((a.ndim - 1,), (0,)), ((), ())), preferred_element_type=F32)


def early_kernel(n, m, at, *refs):
    blocks, factor = refs[: n + m], refs[n + m]
    theirs, own, part, held, right, total, came = refs[n + m + 1 :]
    size, depth = blocks[0].shape
    cols = own.shape[1]
    rows = [pl.ds(pl.multiple_of(at[i] * depth, depth), depth) for i in range(n + m)]
    copies = []
    for i in range(n + m):
        copies.append([pltpu.make_async_copy(blocks[i], held.at[i], came.at[2 * i])])
        if i < n:
            copies[i].append(pltpu.make_async_copy(factor.at[rows[i]], right.at[rows[i]], came.at[2 * i + 1]))
    for copy in sum(copies, []):
        copy.start()
    step = min(256, cols)
    for lo, hi in ((0, n // 2), (n // 2, n), (n, n + m)):
        for copy in sum(copies[lo:hi], []):
            copy.wait()
        for c in range(0, 2 * cols, step):
            here = slice(c, c + step)
            value = None
            for i in range(lo, hi):
                more = dot(held[i], right[rows[i], here])
                value = more if value is None else value + more
            if lo == 0:
                total[:, here] = value
            elif hi > n:
                part[:, here] = value
            elif c < cols:
                own[:, here] = total[:, here] + value
            else:
                theirs[:, c - cols : c - cols + step] = (total[:, here] + value).astype(BF16)


def early(odd, even, factor, at):
    n, m = len(odd), len(even)
    size, depth = odd[0].shape
    wide = factor.shape[1]
    return pl.pallas_call(
        lambda *refs: early_kernel(n, m, *refs),
        out_shape=(
            jax.ShapeDtypeStruct((size, wide // 2), BF16),
            jax.ShapeDtypeStruct((size, wide // 2), F32),
            jax.ShapeDtypeStruct((size, wide), F32),
        ),
        in_specs=[pl.BlockSpec(memory_space=pltpu.SMEM)] + [pl.BlockSpec(memory_space=pl.ANY)] * (n + m + 1),
        out_specs=(pl.BlockSpec(memory_space=pltpu.VMEM),) * 3,
        scratch_shapes=[
            pltpu.VMEM((n + m, size, depth), BF16),
            pltpu.VMEM(factor.shape, BF16),
            pltpu.VMEM((size, wide), F32),
            pltpu.SemaphoreType.DMA((2 * (n + m),)),
        ],
        compiler_params=pltpu.CompilerParams(vmem_limit_bytes=56 * 2**20),
        cost_estimate=pl.CostEstimate(
            flops=2 * (n + m) * size * depth * wide, bytes_accessed=12 * 2**20, transcendentals=0
        ),
    )(jnp.stack(at).astype(jnp.int32), *odd, *even, factor)


def body(weight, anchor, input_factor, output_factor, task_grad):
    y, xh, xl, z, core = (lax.axis_index(a) for a in ROW + COL)
    change = (weight.astype(F32) - anchor.astype(F32)).astype(BF16)
    rows, cols = weight.shape
    half = rows // 2

    depth = input_factor.shape[0] // 2
    mine = lax.dynamic_slice_in_dim(input_factor, core * depth, depth, 0)
    other = lax.dynamic_slice_in_dim(input_factor, (1 - core) * depth, depth, 0)
    pair = jnp.concatenate([mine, shift(other, "core", 1)], axis=1)
    factor = lax.all_gather(pair, "y", axis=0, tiled=True)

    moves = part_ways(output_factor, lambda xh, xl, z: z & 1 != xh, lambda xh, xl, z: (xh, 1 - xl, z ^ 1))
    b, moves = together(turn(change), moves)
    moves = part_ways(moves, lambda xh, xl, z: z & 1 == xh, lambda xh, xl, z: (1 - xh, 1 - xl, z))
    bm, bp, a, moves = together(shift(b, "z", 1), shift(b, "z", -1), shift(b, "xl", 1), moves)
    am, ap, b2 = together(shift(bm, "xl", 1), shift(a, "z", -1), shift(bm, "z", 1))
    same = (z & 1) == xh
    turned = jnp.where(same, output_factor, moves)
    a2, part = together(shift(am, "z", 1), shift(after(turned, factor), "xl", 1))

    def place(dxl, dz):
        return (xl ^ dxl) * 2 + (((z + dz) & 3) >> 1)

    at = [place(0, -1), place(0, 1), place(1, -1), place(1, 1), place(0, 0), place(1, 0), place(1, 2)]
    theirs, own, even = early([am, ap, bm, bp], [a, b, b2], factor, at)
    part = jnp.concatenate([after(part, own), turned], axis=0)
    left = lax.all_gather(part, ("core", "z"), axis=0)

    def more(v, side):
        right = lax.dynamic_slice(factor, (place(0, 2) * depth, side * cols), (depth, cols))
        return even[:, side * cols : (side + 1) * cols] + dot(v, right)

    even_theirs = more(a2, 1).astype(BF16)
    theirs = [after(theirs, even_theirs), even_theirs]
    own = [own, *together(more(after(a2, even_theirs), 0))]
    odd, even = [v + shift(w, "core", 1).astype(F32) for v, w in zip(own, theirs)]
    top, rest = slice(half), slice(half, rows)
    first, second = [jnp.where(same, odd[r], even[r]).astype(BF16) for r in (top, rest)]
    first = shift(first, "xh", 1)
    second = shift(after(second, first), "xh", 1)
    keep = jnp.where(same, even, odd)

    grad, first = together(task_grad.astype(F32), first)
    p = [(keep[top] + first.astype(F32)).astype(BF16)]
    below, above = [shift(p[0], "y", 1)], [shift(p[0], "y", -1)]
    second, above[0] = together(second, above[0])
    p.append((keep[rest] + second.astype(F32)).astype(BF16))
    below.append(shift(p[1], "y", 1))
    above.append(shift(p[1], "y", -1))
    beyond = [shift(below[0], "y", 1), shift(above[1], "y", -1)]

    def share(blocks, dy):
        at = (y + dy) & 3
        size = (2, rows, half)
        corners = [(4 * h + (at & 1) * 2, (1 ^ (at >> 1) ^ xl) * rows, 0) for h in range(2)]
        terms = [dot(lax.dynamic_slice(left, c, size), v) for c, v in zip(corners, blocks)]
        return terms[0] + terms[1]

    penalty = ((share(p, 0) + share(below, -1)) + share(above, 1)) + share(beyond, 2)
    penalty = penalty.astype(BF16).reshape(2 * rows, cols)
    owned = lax.all_to_all(penalty, ("xh",) + COL, split_axis=0, concat_axis=0, tiled=True)
    owned = owned.reshape(2, 16, task_grad.shape[0], cols).astype(F32).sum(axis=0)
    owned = owned.transpose(1, 0, 2).reshape(task_grad.shape)
    return (grad + owned).astype(BF16)


def solution(mesh):
    fine = Mesh(mesh.devices.reshape(4, 2, 2, 4, 2), ROW + COL)
    cut = P(ROW, COL)
    placed = (cut, cut, cut, cut, P(ROW + COL, None))
    return jax.shard_map(
        body, mesh=fine, in_specs=placed, out_specs=P(ROW + COL, None), check_vma=False
    )
```

```python
import jax
import jax.numpy as jnp
from jax import lax
from jax.experimental import pallas as pl
from jax.experimental.pallas import tpu as pltpu
from jax.sharding import Mesh, PartitionSpec as P

ROW = ("y", "xh")
COL = ("xl", "z", "core")
F32, BF16 = jnp.float32, jnp.bfloat16


def shift(v, axis, by):
    n = lax.axis_size(axis)
    return lax.ppermute(v, axis, [(i, (i + by) % n) for i in range(n)])


def turn(v):
    pairs = []
    for xh in range(2):
        for xl in range(2):
            for z in range(4):
                to = ((z & 1) * 2 + 1 - xl) * 4 + (z & ~1) + xh
                pairs.append(((xh * 2 + xl) * 4 + z, to))
    return lax.ppermute(v, ("xh", "xl", "z"), pairs)


def part_ways(v, where, to):
    every = [(xh, xl, z) for xh in range(2) for xl in range(2) for z in range(4)]
    pairs = [(p, to(*p)) for p in every if where(*p)]
    return lax.ppermute(v, ("xh", "xl", "z"), [tuple((q[0] * 2 + q[1]) * 4 + q[2] for q in pair) for pair in pairs])


def after(v, *done):
    return lax.optimization_barrier((v, *done))[0]


def together(*arrays):
    return lax.optimization_barrier(arrays)


def dot(a, b):
    return lax.dot_general(a, b, (((a.ndim - 1,), (0,)), ((), ())), preferred_element_type=F32)


def early_kernel(n, m, at, *refs):
    blocks, factor = refs[: n + m], refs[n + m]
    theirs, own, part, held, right, total, came = refs[n + m + 1 :]
    size, depth = blocks[0].shape
    cols = own.shape[1]
    rows = [pl.ds(pl.multiple_of(at[i] * depth, depth), depth) for i in range(n + m)]
    copies = []
    for i in range(n + m):
        copies.append([pltpu.make_async_copy(blocks[i], held.at[i], came.at[2 * i])])
        if i < n:
            copies[i].append(pltpu.make_async_copy(factor.at[rows[i]], right.at[rows[i]], came.at[2 * i + 1]))
    for copy in sum(copies, []):
        copy.start()
    step = min(256, cols)
    for lo, hi in ((0, n // 2), (n // 2, n), (n, n + m)):
        for copy in sum(copies[lo:hi], []):
            copy.wait()
        for c in range(0, 2 * cols, step):
            here = slice(c, c + step)
            value = None
            for i in range(lo, hi):
                more = dot(held[i], right[rows[i], here])
                value = more if value is None else value + more
            if lo == 0:
                total[:, here] = value
            elif hi > n:
                part[:, here] = value
            elif c < cols:
                own[:, here] = total[:, here] + value
            else:
                theirs[:, c - cols : c - cols + step] = (total[:, here] + value).astype(BF16)


def early(odd, even, factor, at):
    n, m = len(odd), len(even)
    size, depth = odd[0].shape
    wide = factor.shape[1]
    return pl.pallas_call(
        lambda *refs: early_kernel(n, m, *refs),
        out_shape=(
            jax.ShapeDtypeStruct((size, wide // 2), BF16),
            jax.ShapeDtypeStruct((size, wide // 2), F32),
            jax.ShapeDtypeStruct((size, wide), F32),
        ),
        in_specs=[pl.BlockSpec(memory_space=pltpu.SMEM)] + [pl.BlockSpec(memory_space=pl.ANY)] * (n + m + 1),
        out_specs=(pl.BlockSpec(memory_space=pltpu.VMEM),) * 3,
        scratch_shapes=[
            pltpu.VMEM((n + m, size, depth), BF16),
            pltpu.VMEM(factor.shape, BF16),
            pltpu.VMEM((size, wide), F32),
            pltpu.SemaphoreType.DMA((2 * (n + m),)),
        ],
        compiler_params=pltpu.CompilerParams(vmem_limit_bytes=52 * 2**20),
        cost_estimate=pl.CostEstimate(
            flops=2 * (n + m) * size * depth * wide, bytes_accessed=12 * 2**20, transcendentals=0
        ),
    )(jnp.stack(at).astype(jnp.int32), *odd, *even, factor)


def body(weight, anchor, input_factor, output_factor, task_grad):
    y, xh, xl, z, core = (lax.axis_index(a) for a in ROW + COL)
    change = (weight.astype(F32) - anchor.astype(F32)).astype(BF16)
    rows, cols = weight.shape
    half = rows // 2

    depth = input_factor.shape[0] // 2
    mine = lax.dynamic_slice_in_dim(input_factor, core * depth, depth, 0)
    other = lax.dynamic_slice_in_dim(input_factor, (1 - core) * depth, depth, 0)
    pair = jnp.concatenate([mine, shift(other, "core", 1)], axis=1)
    factor = lax.all_gather(pair, "y", axis=0, tiled=True)

    moves = part_ways(output_factor, lambda xh, xl, z: z & 1 != xh, lambda xh, xl, z: (xh, 1 - xl, z ^ 1))
    b, moves = together(turn(change), moves)
    moves = part_ways(moves, lambda xh, xl, z: z & 1 == xh, lambda xh, xl, z: (1 - xh, 1 - xl, z))
    bm, bp, a, moves = together(shift(b, "z", 1), shift(b, "z", -1), shift(b, "xl", 1), moves)
    am, ap, b2 = together(shift(bm, "xl", 1), shift(a, "z", -1), shift(bm, "z", 1))
    same = (z & 1) == xh
    turned = jnp.where(same, output_factor, moves)
    a2, part = together(shift(am, "z", 1), shift(after(turned, factor), "xl", 1))

    def place(dxl, dz):
        return (xl ^ dxl) * 2 + (((z + dz) & 3) >> 1)

    at = [place(0, -1), place(0, 1), place(1, -1), place(1, 1), place(0, 0), place(1, 0), place(1, 2)]
    theirs, own, even = early([am, ap, bm, bp], [a, b, b2], factor, at)
    part = jnp.concatenate([after(part, own), turned], axis=0)
    left = lax.all_gather(part, ("core", "z"), axis=0)

    def more(v, side):
        right = lax.dynamic_slice(factor, (place(0, 2) * depth, side * cols), (depth, cols))
        return even[:, side * cols : (side + 1) * cols] + dot(v, right)

    even_theirs = more(a2, 1).astype(BF16)
    theirs = [after(theirs, even_theirs), even_theirs]
    own = [own, *together(more(after(a2, even_theirs), 0))]
    odd, even = [v + shift(w, "core", 1).astype(F32) for v, w in zip(own, theirs)]
    top, rest = slice(half), slice(half, rows)
    first, second = [jnp.where(same, odd[r], even[r]).astype(BF16) for r in (top, rest)]
    first = shift(first, "xh", 1)
    second = shift(after(second, first), "xh", 1)
    keep = jnp.where(same, even, odd)

    grad, first = together(task_grad.astype(F32), first)
    p = [(keep[top] + first.astype(F32)).astype(BF16)]
    below, above = [shift(p[0], "y", 1)], [shift(p[0], "y", -1)]
    second, above[0] = together(second, above[0])
    p.append((keep[rest] + second.astype(F32)).astype(BF16))
    below.append(shift(p[1], "y", 1))
    above.append(shift(p[1], "y", -1))
    beyond = [shift(below[0], "y", 1), shift(above[1], "y", -1)]

    def share(blocks, dy):
        at = (y + dy) & 3
        size = (2, rows, half)
        corners = [(4 * h + (at & 1) * 2, (1 ^ (at >> 1) ^ xl) * rows, 0) for h in range(2)]
        terms = [dot(lax.dynamic_slice(left, c, size), v) for c, v in zip(corners, blocks)]
        return terms[0] + terms[1]

    penalty = ((share(p, 0) + share(below, -1)) + share(above, 1)) + share(beyond, 2)
    penalty = penalty.astype(BF16).reshape(2 * rows, cols)
    owned = lax.all_to_all(penalty, ("xh",) + COL, split_axis=0, concat_axis=0, tiled=True)
    owned = owned.reshape(2, 16, task_grad.shape[0], cols).astype(F32).sum(axis=0)
    owned = owned.transpose(1, 0, 2).reshape(task_grad.shape)
    return (grad + owned).astype(BF16)


def solution(mesh):
    fine = Mesh(mesh.devices.reshape(4, 2, 2, 4, 2), ROW + COL)
    cut = P(ROW, COL)
    placed = (cut, cut, cut, cut, P(ROW + COL, None))
    return jax.shard_map(
        body, mesh=fine, in_specs=placed, out_specs=P(ROW + COL, None), check_vma=False
    )
```

```python
import jax
import jax.numpy as jnp
from jax import lax
from jax.experimental import pallas as pl
from jax.experimental.pallas import tpu as pltpu
from jax.sharding import Mesh, PartitionSpec as P

ROW = ("y", "xh")
COL = ("xl", "z", "core")
F32, BF16 = jnp.float32, jnp.bfloat16


def shift(v, axis, by):
    n = lax.axis_size(axis)
    return lax.ppermute(v, axis, [(i, (i + by) % n) for i in range(n)])


def turn(v):
    pairs = []
    for xh in range(2):
        for xl in range(2):
            for z in range(4):
                to = ((z & 1) * 2 + 1 - xl) * 4 + (z & ~1) + xh
                pairs.append(((xh * 2 + xl) * 4 + z, to))
    return lax.ppermute(v, ("xh", "xl", "z"), pairs)


def part_ways(v, where, to):
    every = [(xh, xl, z) for xh in range(2) for xl in range(2) for z in range(4)]
    pairs = [(p, to(*p)) for p in every if where(*p)]
    return lax.ppermute(v, ("xh", "xl", "z"), [tuple((q[0] * 2 + q[1]) * 4 + q[2] for q in pair) for pair in pairs])


def after(v, *done):
    return lax.optimization_barrier((v, *done))[0]


def together(*arrays):
    return lax.optimization_barrier(arrays)


def dot(a, b):
    return lax.dot_general(a, b, (((a.ndim - 1,), (0,)), ((), ())), preferred_element_type=F32)


def early_kernel(n, m, at, *refs):
    blocks, factor = refs[: n + m], refs[n + m]
    theirs, own, part, held, right, total, came = refs[n + m + 1 :]
    size, depth = blocks[0].shape
    cols = own.shape[1]
    rows = [pl.ds(pl.multiple_of(at[i] * depth, depth), depth) for i in range(n + m)]
    copies = []
    for i in range(n + m):
        copies.append([pltpu.make_async_copy(blocks[i], held.at[i], came.at[2 * i])])
        if i < n:
            copies[i].append(pltpu.make_async_copy(factor.at[rows[i]], right.at[rows[i]], came.at[2 * i + 1]))
    for copy in sum(copies, []):
        copy.start()
    step = min(256, cols)
    for lo, hi in ((0, n // 2), (n // 2, n), (n, n + m)):
        for copy in sum(copies[lo:hi], []):
            copy.wait()
        for c in range(0, 2 * cols, step):
            here = slice(c, c + step)
            value = None
            for i in range(lo, hi):
                more = dot(held[i], right[rows[i], here])
                value = more if value is None else value + more
            if lo == 0:
                total[:, here] = value
            elif hi > n:
                part[:, here] = value
            elif c < cols:
                own[:, here] = total[:, here] + value
            else:
                theirs[:, c - cols : c - cols + step] = (total[:, here] + value).astype(BF16)


def early(odd, even, factor, at):
    n, m = len(odd), len(even)
    size, depth = odd[0].shape
    wide = factor.shape[1]
    return pl.pallas_call(
        lambda *refs: early_kernel(n, m, *refs),
        out_shape=(
            jax.ShapeDtypeStruct((size, wide // 2), BF16),
            jax.ShapeDtypeStruct((size, wide // 2), F32),
            jax.ShapeDtypeStruct((size, wide), F32),
        ),
        in_specs=[pl.BlockSpec(memory_space=pltpu.SMEM)] + [pl.BlockSpec(memory_space=pl.ANY)] * (n + m + 1),
        out_specs=(pl.BlockSpec(memory_space=pltpu.VMEM),) * 3,
        scratch_shapes=[
            pltpu.VMEM((n + m, size, depth), BF16),
            pltpu.VMEM(factor.shape, BF16),
            pltpu.VMEM((size, wide), F32),
            pltpu.SemaphoreType.DMA((2 * (n + m),)),
        ],
        compiler_params=pltpu.CompilerParams(vmem_limit_bytes=52 * 2**20),
        cost_estimate=pl.CostEstimate(
            flops=2 * (n + m) * size * depth * wide, bytes_accessed=12 * 2**20, transcendentals=0
        ),
    )(jnp.stack(at).astype(jnp.int32), *odd, *even, factor)


def body(weight, anchor, input_factor, output_factor, task_grad):
    y, xh, xl, z, core = (lax.axis_index(a) for a in ROW + COL)
    change = (weight.astype(F32) - anchor.astype(F32)).astype(BF16)
    rows, cols = weight.shape
    half = rows // 2

    depth = input_factor.shape[0] // 2
    mine = lax.dynamic_slice_in_dim(input_factor, core * depth, depth, 0)
    other = lax.dynamic_slice_in_dim(input_factor, (1 - core) * depth, depth, 0)
    pair = jnp.concatenate([mine, shift(other, "core", 1)], axis=1)
    factor = lax.all_gather(pair, "y", axis=0, tiled=True)

    moves = part_ways(output_factor, lambda xh, xl, z: z & 1 != xh, lambda xh, xl, z: (xh, 1 - xl, z ^ 1))
    b, moves = together(turn(change), moves)
    moves = part_ways(moves, lambda xh, xl, z: z & 1 == xh, lambda xh, xl, z: (1 - xh, 1 - xl, z))
    bm, bp, a, moves = together(shift(b, "z", 1), shift(b, "z", -1), shift(b, "xl", 1), moves)
    am, ap, b2 = together(shift(bm, "xl", 1), shift(a, "z", -1), shift(bm, "z", 1))
    same = (z & 1) == xh
    turned = jnp.where(same, output_factor, moves)
    a2, part = shift(am, "z", 1), shift(turned, "xl", 1)

    def place(dxl, dz):
        return (xl ^ dxl) * 2 + (((z + dz) & 3) >> 1)

    at = [place(0, -1), place(0, 1), place(1, -1), place(1, 1), place(0, 0), place(1, 0), place(1, 2)]
    theirs, own, even = early([am, ap, bm, bp], [a, b, b2], factor, at)
    a2, part, own = together(a2, part, own)
    part = jnp.concatenate([part, turned], axis=0)
    left = lax.all_gather(part, ("core", "z"), axis=0)

    def more(v, side):
        right = lax.dynamic_slice(factor, (place(0, 2) * depth, side * cols), (depth, cols))
        return even[:, side * cols : (side + 1) * cols] + dot(v, right)

    even_theirs = more(a2, 1).astype(BF16)
    theirs = [after(theirs, even_theirs), even_theirs]
    own = [own, *together(more(after(a2, even_theirs), 0))]
    odd, even = [v + shift(w, "core", 1).astype(F32) for v, w in zip(own, theirs)]
    top, rest = slice(half), slice(half, rows)
    first, second = [jnp.where(same, odd[r], even[r]).astype(BF16) for r in (top, rest)]
    first = shift(first, "xh", 1)
    second = shift(after(second, first), "xh", 1)
    keep = jnp.where(same, even, odd)

    grad, first = together(task_grad.astype(F32), first)
    p = [(keep[top] + first.astype(F32)).astype(BF16)]
    below, above = [shift(p[0], "y", 1)], [shift(p[0], "y", -1)]
    second, above[0] = together(second, above[0])
    p.append((keep[rest] + second.astype(F32)).astype(BF16))
    below.append(shift(p[1], "y", 1))
    above.append(shift(p[1], "y", -1))
    beyond = [shift(below[0], "y", 1), shift(above[1], "y", -1)]

    def share(blocks, dy):
        at = (y + dy) & 3
        size = (2, rows, half)
        corners = [(4 * h + (at & 1) * 2, (1 ^ (at >> 1) ^ xl) * rows, 0) for h in range(2)]
        terms = [dot(lax.dynamic_slice(left, c, size), v) for c, v in zip(corners, blocks)]
        return terms[0] + terms[1]

    penalty = ((share(p, 0) + share(below, -1)) + share(above, 1)) + share(beyond, 2)
    penalty = penalty.astype(BF16).reshape(2 * rows, cols)
    owned = lax.all_to_all(penalty, ("xh",) + COL, split_axis=0, concat_axis=0, tiled=True)
    owned = owned.reshape(2, 16, task_grad.shape[0], cols).astype(F32).sum(axis=0)
    owned = owned.transpose(1, 0, 2).reshape(task_grad.shape)
    return (grad + owned).astype(BF16)


def solution(mesh):
    fine = Mesh(mesh.devices.reshape(4, 2, 2, 4, 2), ROW + COL)
    cut = P(ROW, COL)
    placed = (cut, cut, cut, cut, P(ROW + COL, None))
    return jax.shard_map(
        body, mesh=fine, in_specs=placed, out_specs=P(ROW + COL, None), check_vma=False
    )
```
